32 devices in a mesh: wide: 8 (over y, x, core), narrow: 4 (over z).
Axes of the slice: x: 2, y: 2, z: 4, core: 2. Of those that a mesh axis runs over, the one named last changes fastest.
Arguments:
- pixels: bfloat16 [32, 32, 256, 768], P('wide', 'narrow')
- coarse_pixels: bfloat16 [128, 128, 768], P('wide', 'narrow')
- unsure: int32 [32, 32], P('wide', 'narrow'), may hold values from 0 to 1, as said below
- patch_weight: bfloat16 [768, 1024], replicated, may hold values from -0.21875 to 0.21875
- position: bfloat16 [256, 1024], replicated, may hold values from -3 to 3
- qkv_weight: bfloat16 [1024, 3072], replicated
- out_weight: bfloat16 [1024, 1024], replicated, may hold values from -0.1875 to 0.1875
- join_weight: bfloat16 [1024, 1024], replicated, may hold values from -0.1875 to 0.1875
- gain_attn: float32 [1024], replicated, may hold values from 0.25 to 1.75
- gain_head: float32 [1024], replicated, may hold values from 0.25 to 1.75
- head_weight: bfloat16 [1024, 16], replicated, may hold values from -0.1875 to 0.1875
Outputs:
- logits: bfloat16 [32, 32, 16, 256], P('wide', 'narrow')
The draws below stay inside these ranges and needn't reach their ends.
Inputs may be any that keep to these rules, and one draw needn't show every extreme that they name: `unsure`: A device holds at most 25 flagged tiles, and in every column of devices along wide one device holds exactly that many; the devices of one column along wide hold 7 * 8 flagged tiles together.
All inputs are finite; a program needn't handle non-finite values.
Results may differ from the reference program's by a relative error of at most 0.01.
Values may be sent and summed in bfloat16 or wider, within the bound.
A program may use at most 320 MiB of HBM per device.

```python
import math
import jax
import jax.numpy as jnp
from jax import lax

D = 1024
HEADS = 16
HD = 64
PD = 768
CLASSES = 16
TS = 16
TR = 4
TC = 8
TT = 256
CS = 4
TILE_DEV = 32
UNSURE_MOST = 25
RECV = 7
TROWS = 32
TCOLS = 32
CROWS = 128
CCOLS = 128
ESCALATED = 224
N_WIDE = 8
N_NARROW = 4


def draw_pixels(key, part):
    key = jax.random.fold_in(key, 3)
    first, second = jax.random.split(key, 2)
    shape = (TROWS, TCOLS, TT, PD)
    token_shape = (TROWS, TCOLS, TT, 1)
    base = jax.random.normal(first, shape, jnp.float32)
    scale = jnp.exp(jax.random.uniform(second, token_shape, jnp.float32, math.log(0.3), math.log(3.0)))
    values = jnp.clip(base, -5.0, 5.0) * scale
    return values.astype(jnp.bfloat16)


def draw_coarse_pixels(key, part):
    key = jax.random.fold_in(key, 7)
    first, second = jax.random.split(key, 2)
    shape = (CROWS, CCOLS, PD)
    token_shape = (CROWS, CCOLS, 1)
    base = jax.random.normal(first, shape, jnp.float32)
    scale = jnp.exp(jax.random.uniform(second, token_shape, jnp.float32, math.log(0.3), math.log(3.0)))
    values = jnp.clip(base, -5.0, 5.0) * scale
    return values.astype(jnp.bfloat16)


def draw_qkv_weight(key, part):
    key = jax.random.fold_in(key, 5)
    first = jax.random.fold_in(key, 0)
    base = jnp.clip(jax.random.normal(first, (D, 3 * D), jnp.float32), -5.0, 5.0) * D ** (-0.5)
    return base.astype(jnp.bfloat16)


def draw_unsure(key, part):
    key = jax.random.fold_in(key, 11)
    first, second, third = jax.random.split(key, 3)
    extra_total = RECV * N_WIDE - UNSURE_MOST - (N_WIDE - 1)
    cap_extra = UNSURE_MOST // 2
    pool = (N_WIDE - 1) * cap_extra
    hottest = jax.random.randint(first, (N_NARROW,), 0, N_WIDE)
    shuffled = jax.vmap(lambda sub: jax.random.permutation(sub, pool))(jax.random.split(second, N_NARROW))
    owners = shuffled[:, :extra_total] // cap_extra
    others = jnp.sum((owners[:, :, None] == jnp.arange(N_WIDE - 1, dtype=jnp.int32)[None, None, :]).astype(jnp.int32), axis=1) + 1
    wide_pos = jnp.arange(N_WIDE, dtype=jnp.int32)
    lookup = wide_pos[None, :] - (wide_pos[None, :] > hottest[:, None]).astype(jnp.int32)
    lookup = jnp.clip(lookup, 0, N_WIDE - 2)
    taken = jnp.take_along_axis(others, lookup, axis=1)
    counts = jnp.where(wide_pos[None, :] == hottest[:, None], UNSURE_MOST, taken)
    ranks = jax.vmap(lambda sub: jax.random.permutation(sub, TILE_DEV))(jax.random.split(third, N_NARROW * N_WIDE))
    ranks = ranks.reshape(N_NARROW, N_WIDE, TILE_DEV)
    flags = (ranks < counts[:, :, None]).astype(jnp.int32)
    flags = flags.reshape(N_NARROW, N_WIDE, TR, TC).transpose(1, 2, 0, 3)
    return flags.reshape(TROWS, TCOLS)


def scatter_about(key, extent, width, bound, held_as=jnp.bfloat16):
    values = width * jax.random.normal(key, extent, jnp.float32)
    return jnp.clip(values, min=-bound, max=bound).astype(held_as)


def setup_inputs(seed: int = 0) -> dict:
    key_list = jax.random.split(jax.random.key(seed), 12)
    return {
        "pixels": draw_pixels(jax.random.fold_in(key_list[11], 71), 0),
        "coarse_pixels": draw_coarse_pixels(jax.random.fold_in(key_list[11], 71), 0),
        "unsure": draw_unsure(jax.random.fold_in(key_list[11], 71), 0),
        "patch_weight": scatter_about(key_list[3], (PD, D), PD ** -0.5, 0.21875),
        "position": scatter_about(key_list[4], (TT, D), 0.5, 3.0),
        "qkv_weight": draw_qkv_weight(jax.random.fold_in(key_list[11], 71), 0),
        "out_weight": scatter_about(key_list[6], (D, D), D ** -0.5, 0.1875),
        "join_weight": scatter_about(key_list[7], (D, D), D ** -0.5, 0.1875),
        "gain_attn": jnp.clip(1.0 + 0.15 * jax.random.normal(key_list[8], (D,), jnp.float32), 0.25, 1.75),
        "gain_head": jnp.clip(1.0 + 0.15 * jax.random.normal(key_list[9], (D,), jnp.float32), 0.25, 1.75),
        "head_weight": scatter_about(key_list[10], (D, CLASSES), D ** -0.5, 0.1875),
    }


EPS = 1e-06

def interp_table():
    fine = jnp.arange(TS, dtype=jnp.int32)
    eighths = 2 * fine - 3
    lower = eighths // 8
    frac = (eighths - 8 * lower).astype(jnp.float32) / 8.0
    column = jnp.arange(CS + 2, dtype=jnp.int32)
    left = (column[None, :] == (lower + 1)[:, None]).astype(jnp.float32)
    right = (column[None, :] == (lower + 2)[:, None]).astype(jnp.float32)
    return left * (1.0 - frac)[:, None] + right * frac[:, None]

def layer_norm(values, gain):
    center = values - lax.optimization_barrier(jnp.mean(values, axis=-1, keepdims=True))
    spread = lax.optimization_barrier(jnp.mean(center * center, axis=-1, keepdims=True))
    return center * lax.rsqrt(spread + EPS) * gain

def attend(tokens, gain_attn, qkv_weight, out_weight):
    count = tokens.shape[0]
    normed = layer_norm(tokens, gain_attn).astype(jnp.bfloat16).reshape(-1, D)
    packed = jnp.dot(normed, qkv_weight, preferred_element_type=jnp.float32).astype(jnp.bfloat16)
    packed = packed.reshape(count, TT, 3, HEADS, HD)
    queries = packed[:, :, 0].astype(jnp.float32)
    key_rows = packed[:, :, 1].astype(jnp.float32)
    value_rows = packed[:, :, 2].astype(jnp.float32)
    scores = jnp.einsum('nqhd,nkhd->nhqk', queries, key_rows) * HD ** (-0.5)
    weights = jax.nn.softmax(scores, axis=-1).astype(jnp.bfloat16)
    mixed = jnp.einsum('nhqk,nkhd->nqhd', weights.astype(jnp.float32), value_rows)
    mixed = mixed.astype(jnp.bfloat16).reshape(-1, D)
    return tokens + jnp.dot(mixed, out_weight, preferred_element_type=jnp.float32).reshape(count, TT, D)

def reference(pixels, coarse_pixels, unsure, patch_weight, position, qkv_weight, out_weight, join_weight, gain_attn, gain_head, head_weight):
    table = interp_table()
    highest = lax.Precision.HIGHEST
    win_rows = CROWS // TS
    win_cols = CCOLS // TS
    windows = coarse_pixels.reshape(win_rows, TS, win_cols, TS, PD).transpose(0, 2, 1, 3, 4)
    windows = windows.reshape(win_rows, win_cols * TT, PD)

    def glance_band(band):
        embed = jnp.dot(band, patch_weight, preferred_element_type=jnp.float32).reshape(win_cols, TT, D)
        embed = embed + position.astype(jnp.float32)
        return attend(embed, gain_attn, qkv_weight, out_weight).astype(jnp.bfloat16)
    bands = lax.map(glance_band, windows)
    features = bands.reshape(win_rows, win_cols, TS, TS, D).transpose(0, 2, 1, 3, 4).reshape(CROWS, CCOLS, D)
    padded = jnp.pad(features, ((1, 1), (1, 1), (0, 0)), mode='edge')

    def head_row(row):
        normed = layer_norm(row.astype(jnp.float32), gain_head).astype(jnp.bfloat16)
        return jnp.dot(normed, head_weight, preferred_element_type=jnp.float32)
    coarse_logits = lax.map(head_row, padded)
    row_index = (jnp.arange(TROWS, dtype=jnp.int32)[:, None] * CS + jnp.arange(CS + 2, dtype=jnp.int32)[None, :]).reshape(-1)
    col_index = (jnp.arange(TCOLS, dtype=jnp.int32)[:, None] * CS + jnp.arange(CS + 2, dtype=jnp.int32)[None, :]).reshape(-1)
    tile_logits = jnp.take(jnp.take(coarse_logits, row_index, axis=0), col_index, axis=1)
    tile_logits = tile_logits.reshape(TROWS, CS + 2, TCOLS, CS + 2, CLASSES)
    glance_logits = jnp.einsum('pi,qj,aibjc->abcpq', table, table, tile_logits, precision=highest)
    glance_logits = glance_logits.reshape(TROWS * TCOLS, CLASSES, TT)
    flags = unsure.reshape(-1)
    chosen = jnp.nonzero(flags > 0, size=ESCALATED)[0].astype(jnp.int32)
    flat_pixels = pixels.reshape(TROWS * TCOLS, TT, PD)

    def cut_rim(row_start, col_start):
        zero = jnp.zeros((), jnp.int32)
        return lax.dynamic_slice(padded, (row_start.astype(jnp.int32), col_start.astype(jnp.int32), zero), (CS + 2, CS + 2, D))

    def focus_block(block):
        tile_rows = block // TCOLS
        tile_cols = block % TCOLS
        rims = jax.vmap(cut_rim)(tile_rows * CS, tile_cols * CS)
        lifted = jnp.einsum('pi,qj,nijd->npqd', table, table, rims.astype(jnp.float32), precision=highest)
        lifted = lifted.astype(jnp.bfloat16).reshape(-1, D)
        tile_pixels = flat_pixels[block].reshape(-1, PD)
        embed = jnp.dot(tile_pixels, patch_weight, preferred_element_type=jnp.float32)
        embed = embed + jnp.dot(lifted, join_weight, preferred_element_type=jnp.float32)
        embed = embed.reshape(-1, TT, D) + position.astype(jnp.float32)
        result = attend(embed, gain_attn, qkv_weight, out_weight)
        normed = layer_norm(result, gain_head).astype(jnp.bfloat16).reshape(-1, D)
        answer = jnp.dot(normed, head_weight, preferred_element_type=jnp.float32).reshape(-1, TT, CLASSES)
        return answer.transpose(0, 2, 1).astype(jnp.bfloat16)
    focused = lax.map(focus_block, chosen.reshape(-1, 8)).reshape(ESCALATED, CLASSES, TT)
    combined = glance_logits.astype(jnp.bfloat16).at[chosen].set(focused)
    return combined.reshape(TROWS, TCOLS, CLASSES, TT)
```

```python
import functools

import jax
import jax.numpy as jnp
from jax import lax
from jax.experimental import pallas as pl
from jax.experimental.pallas import tpu as pltpu
from jax.sharding import PartitionSpec as P

D = 1024
HEADS = 16
HD = 64
PD = 768
CLASSES = 16
TS = 16
TT = 256
CS = 4
UNSURE_MOST = 25
RECV = 7


EPS = 1e-06


def padded(cells, sides, width):
    for axis, dim in sides:
        count = lax.axis_size(axis)
        ends = count - 1
        head = lax.slice_in_dim(cells, 0, width, axis=dim)
        tail = lax.slice_in_dim(cells, cells.shape[dim] - width, cells.shape[dim], axis=dim)
        cells = jnp.concatenate(
            [
                lax.ppermute(tail, axis, [(i, (i + 1) % count) for i in range(ends)]),
                cells,
                lax.ppermute(head, axis, [((i + 1) % count, i) for i in range(ends)]),
            ],
            axis=dim,
        )
    return cells


def carried_in(x, axis, combine, identity):
    count, position = (lax.axis_size(axis), lax.axis_index(axis))
    everything = lax.all_gather(x, axis)
    start = jnp.broadcast_to(jnp.asarray(identity, x.dtype), x.shape)

    def step(k, before):
        reached = k < position
        new = combine(before, everything[k])
        return jnp.where(reached, new, before)

    return lax.fori_loop(0, count, step, start)


def interp_table():
    fine = jnp.arange(TS, dtype=jnp.int32)
    eighths = 2 * fine - 3
    lower = eighths // 8
    frac = (eighths - 8 * lower).astype(jnp.float32) / 8.0
    column = jnp.arange(CS + 2, dtype=jnp.int32)
    left = (column[None, :] == (lower + 1)[:, None]).astype(jnp.float32)
    right = (column[None, :] == (lower + 2)[:, None]).astype(jnp.float32)
    return left * (1.0 - frac)[:, None] + right * frac[:, None]


def layer_norm(values, gain):
    center = values - jnp.mean(values, axis=-1, keepdims=True)
    spread = jnp.mean(center * center, axis=-1, keepdims=True)
    return center * lax.rsqrt(spread + EPS) * gain


RIM = 48
RIM_USED = (CS + 2) * (CS + 2)
LOG2E = 1.4426950408889634
VMEM_BYTES = 56 * 1024 * 1024


def dot(a, b):
    return jnp.dot(a, b, preferred_element_type=jnp.float32)


def dot_t(a, b):
    return lax.dot_general(a, b, (((1,), (1,)), ((), ())), preferred_element_type=jnp.float32)


def attend_tile(tokens, gain_ref, qkv_ref, out_ref, mixed_ref):
    normed = layer_norm(tokens, gain_ref[...]).astype(jnp.bfloat16)
    lane = lax.broadcasted_iota(jnp.int32, (TT, 2 * HD), 1)
    first = lane < HD
    ones_a = jnp.where(first, 1.0, 0.0).astype(jnp.bfloat16)
    ones_b = jnp.where(first, 0.0, 1.0).astype(jnp.bfloat16)
    zero = jnp.zeros((TT, 2 * HD), jnp.bfloat16)
    wide = 4 * HD
    for group in range(D // wide):
        at = group * wide
        q = dot(normed, qkv_ref[:, at : at + wide]).astype(jnp.bfloat16)
        k = dot(normed, qkv_ref[:, D + at : D + at + wide]).astype(jnp.bfloat16)
        v = dot(normed, qkv_ref[:, 2 * D + at : 2 * D + at + wide]).astype(jnp.bfloat16)
        for pair in range(2):
            cols = slice(pair * 2 * HD, (pair + 1) * 2 * HD)
            q2, k2, v2 = q[:, cols], k[:, cols], v[:, cols]
            parts = []
            for mine in (first, ~first):
                s = dot_t(jnp.where(mine, q2, zero), k2)
                top = jnp.max(s, axis=-1, keepdims=True)
                parts.append(jnp.exp2((s - top) * (LOG2E * HD ** (-0.5))).astype(jnp.bfloat16))
            p = jnp.concatenate(parts, axis=1)
            upper = jnp.concatenate([jnp.where(first, v2, zero), ones_a], axis=1)
            lower = jnp.concatenate([jnp.where(first, zero, v2), ones_b], axis=1)
            o = dot(p, jnp.concatenate([upper, lower], axis=0))
            mixed_ref[:, at + pair * 2 * HD : at + (pair + 1) * 2 * HD] = (
                o[:, : 2 * HD] / o[:, 2 * HD :]
            ).astype(jnp.bfloat16)
    return tokens + dot(mixed_ref[...], out_ref[...])


def glance_kernel(px_ref, patch_ref, pos_ref, gain_ref, qkv_ref, out_ref, feat_ref, mixed_ref):
    patches = px_ref[...].reshape(TT, PD)
    embed = dot(patches, patch_ref[...]) + pos_ref[...].astype(jnp.float32)
    result = attend_tile(embed, gain_ref, qkv_ref, out_ref, mixed_ref)
    feat_ref[...] = result.astype(jnp.bfloat16).reshape(feat_ref.shape)


def fixed(shape):
    return pl.BlockSpec(
        shape, lambda *_: (0,) * len(shape), pipeline_mode=pl.Buffered(1)
    )


def glance(coarse, patch_weight, position, gain_attn, qkv_weight, out_weight):
    rows, cols, _ = coarse.shape
    count = (rows // TS) * (cols // TS)
    return pl.pallas_call(
        glance_kernel,
        grid=(rows // TS, cols // TS),
        in_specs=[
            pl.BlockSpec((TS, TS, PD), lambda a, b: (a, b, 0)),
            fixed((PD, D)),
            fixed((TT, D)),
            fixed((1, D)),
            fixed((D, 3 * D)),
            fixed((D, D)),
        ],
        out_specs=pl.BlockSpec((TS, TS, D), lambda a, b: (a, b, 0)),
        out_shape=jax.ShapeDtypeStruct((rows, cols, D), jnp.bfloat16),
        scratch_shapes=[pltpu.VMEM((TT, D), jnp.bfloat16)],
        compiler_params=pltpu.CompilerParams(vmem_limit_bytes=VMEM_BYTES),
        cost_estimate=pl.CostEstimate(
            flops=count * 4_000_000_000, bytes_accessed=14_000_000, transcendentals=0
        ),
    )(coarse, patch_weight, position, gain_attn.reshape(1, D), qkv_weight, out_weight)


def focus_kernel(
    where_ref,
    px_ref,
    rim_ref,
    lift_ref,
    patch_ref,
    join_ref,
    pos_ref,
    gain_ref,
    qkv_ref,
    out_ref,
    gain_head_ref,
    head_ref,
    answer_ref,
    mixed_ref,
):
    joined = dot(rim_ref[0], join_ref[...])
    high = joined.astype(jnp.bfloat16)
    low = (joined - high.astype(jnp.float32)).astype(jnp.bfloat16)
    embed = dot(px_ref[0], patch_ref[...])
    embed = embed + dot(lift_ref[...], jnp.concatenate([high, low], axis=0))
    embed = embed + pos_ref[...].astype(jnp.float32)
    result = attend_tile(embed, gain_ref, qkv_ref, out_ref, mixed_ref)
    normed = layer_norm(result, gain_head_ref[...]).astype(jnp.bfloat16)
    answer_ref[0] = dot_t(head_ref[...], normed).astype(jnp.bfloat16)


def focus(where_from, pixels, rims, lift, weights):
    patch_weight, join_weight, position, gain_attn, qkv_weight, out_weight, gain_head, head_t = weights
    count = where_from.shape[0]
    return pl.pallas_call(
        focus_kernel,
        grid_spec=pltpu.PrefetchScalarGridSpec(
            num_scalar_prefetch=1,
            grid=(count,),
            in_specs=[
                pl.BlockSpec((1, TT, PD), lambda i, w: (w[i], 0, 0)),
                pl.BlockSpec((1, RIM, D), lambda i, w: (w[i], 0, 0)),
                fixed((TT, 2 * RIM)),
                fixed((PD, D)),
                fixed((D, D)),
                fixed((TT, D)),
                fixed((1, D)),
                fixed((D, 3 * D)),
                fixed((D, D)),
                fixed((1, D)),
                fixed((CLASSES, D)),
            ],
            out_specs=pl.BlockSpec((1, CLASSES, TT), lambda i, w: (i, 0, 0)),
            scratch_shapes=[pltpu.VMEM((TT, D), jnp.bfloat16)],
        ),
        out_shape=jax.ShapeDtypeStruct((count, CLASSES, TT), jnp.bfloat16),
        compiler_params=pltpu.CompilerParams(vmem_limit_bytes=VMEM_BYTES),
        cost_estimate=pl.CostEstimate(
            flops=count * 4_500_000_000, bytes_accessed=20_000_000, transcendentals=0
        ),
    )(
        where_from,
        pixels,
        rims,
        lift,
        patch_weight,
        join_weight,
        position,
        gain_attn.reshape(1, D),
        qkv_weight,
        out_weight,
        gain_head.reshape(1, D),
        head_t,
    )


def lift_table():
    table = interp_table()
    both = (table[:, None, :, None] * table[None, :, None, :]).reshape(TT, RIM_USED)
    return jnp.pad(both, ((0, 0), (0, RIM - RIM_USED))).astype(jnp.bfloat16)


def rim_cells(tiles, tile_cols, cols):
    k = jnp.arange(RIM, dtype=jnp.int32)
    cell = (tiles // tile_cols * CS)[:, None] + k[None, :] // (CS + 2)
    cell = cell * cols + (tiles % tile_cols * CS)[:, None] + k[None, :] % (CS + 2)
    return jnp.where(k[None, :] < RIM_USED, cell, -1)


def bordered_features(features):
    bordered = padded(features, (("wide", 0), ("narrow", 1)), 1)
    wide_pos = lax.axis_index("wide")
    narrow_pos = lax.axis_index("narrow")
    top_row = jnp.where(wide_pos == 0, bordered[1:2], bordered[0:1])
    bottom_row = jnp.where(
        wide_pos == lax.axis_size("wide") - 1, bordered[-2:-1], bordered[-1:]
    )
    bordered = jnp.concatenate([top_row, bordered[1:-1], bottom_row], axis=0)
    left_col = jnp.where(narrow_pos == 0, bordered[:, 1:2], bordered[:, 0:1])
    right_col = jnp.where(
        narrow_pos == lax.axis_size("narrow") - 1, bordered[:, -2:-1], bordered[:, -1:]
    )
    bordered = jnp.concatenate([left_col, bordered[:, 1:-1], right_col], axis=1)
    return bordered


def glance_answer(flat, gain_head, head_weight, cells, lift):
    tile_count = cells.shape[0]
    normed = layer_norm(flat.astype(jnp.float32), gain_head).astype(jnp.bfloat16)
    coarse = lax.dot_general(
        head_weight, normed, (((0,), (1,)), ((), ())), preferred_element_type=jnp.float32
    )
    pieces = []
    for _ in range(3):
        piece = lax.reduce_precision(coarse, 8, 7)
        pieces.append(piece.astype(jnp.bfloat16))
        coarse = coarse - piece
    stacked = jnp.concatenate(pieces, axis=0)
    chosen = (
        jnp.arange(flat.shape[0], dtype=jnp.int32)[:, None] == cells.reshape(1, -1)
    ).astype(jnp.bfloat16)
    rim_logits = dot(stacked, chosen).astype(jnp.bfloat16).reshape(3 * CLASSES * tile_count, RIM)
    fine = dot_t(rim_logits, lift).reshape(3, CLASSES, tile_count, TT)
    return (fine[0] + fine[1] + fine[2]).astype(jnp.bfloat16).transpose(1, 0, 2)


def per_device(
    pixels,
    coarse_pixels,
    unsure,
    patch_weight,
    position,
    qkv_weight,
    out_weight,
    join_weight,
    gain_attn,
    gain_head,
    head_weight,
):
    tile_rows, tile_cols = unsure.shape
    tile_count = tile_rows * tile_cols
    wide_pos = lax.axis_index("wide")
    wide_len = lax.axis_size("wide")
    flags = unsure.reshape(-1)
    flat_pixels = pixels.reshape(tile_count, TT, PD)
    positions = jnp.arange(tile_count, dtype=jnp.int32)
    capacity = max(2, (UNSURE_MOST + wide_len - 1) // wide_len)
    slot_total = wide_len * capacity
    local_count = jnp.sum(flags)
    before = carried_in(local_count, "wide", jnp.add, jnp.zeros((), jnp.int32))
    order = jnp.cumsum(flags) - flags
    target = (before + order) % wide_len
    same = (
        (target[:, None] == target[None, :])
        & (positions[None, :] < positions[:, None])
        & (flags[None, :] == 1)
    )
    depth = jnp.sum(same.astype(jnp.int32), axis=1)
    slot = target * capacity + depth
    slot_ids = jnp.arange(slot_total, dtype=jnp.int32)
    choose = ((flags[None, :] == 1) & (slot[None, :] == slot_ids[:, None])).astype(jnp.int32)
    source = jnp.sum(choose * positions[None, :], axis=1)
    filled = jnp.sum(choose, axis=1)
    exchange = functools.partial(
        lax.all_to_all, axis_name="wide", split_axis=0, concat_axis=0, tiled=True
    )
    got_pixels = exchange(flat_pixels[source])
    got_fill = exchange(filled.astype(jnp.bfloat16).reshape(wide_len, capacity))
    features = glance(coarse_pixels, patch_weight, position, gain_attn, qkv_weight, out_weight)
    bordered = bordered_features(features)
    cols = bordered.shape[1]
    flat = bordered.reshape(-1, D)
    lift = lift_table()
    cells = rim_cells(positions, tile_cols, cols)
    send_cells = rim_cells(source, tile_cols, cols).reshape(-1)
    chosen = (
        send_cells[:, None] == jnp.arange(flat.shape[0], dtype=jnp.int32)[None, :]
    ).astype(jnp.bfloat16)
    got_side = exchange(dot(chosen, flat).astype(jnp.bfloat16).reshape(slot_total, RIM, D))
    glance_logits = glance_answer(flat, gain_head, head_weight, cells, lift)
    present = got_fill.reshape(-1).astype(jnp.int32)
    place = jnp.cumsum(present) - present
    pick = (present[None, :] == 1) & (place[None, :] == jnp.arange(RECV, dtype=jnp.int32)[:, None])
    where_from = jnp.sum(pick.astype(jnp.int32) * slot_ids[None, :], axis=1)
    weights = (
        patch_weight,
        join_weight,
        position,
        gain_attn,
        qkv_weight,
        out_weight,
        gain_head,
        head_weight.T,
    )
    answer = focus(
        where_from, got_pixels, got_side, jnp.concatenate([lift, lift], axis=1), weights
    )
    back = dot(
        pick.astype(jnp.bfloat16).T, answer.reshape(RECV, CLASSES * TT)
    ).astype(jnp.bfloat16)
    returned = exchange(back.reshape(slot_total, CLASSES, TT))
    focused = returned[jnp.clip(slot, 0, slot_total - 1)]
    result = jnp.where(flags[:, None, None] == 1, focused, glance_logits)
    return result.reshape(tile_rows, tile_cols, CLASSES, TT)


def solution(mesh):
    return jax.shard_map(
        per_device,
        mesh=mesh,
        in_specs=(
            P("wide", "narrow", None, None),
            P("wide", "narrow", None),
            P("wide", "narrow"),
            P(),
            P(),
            P(),
            P(),
            P(),
            P(),
            P(),
            P(),
        ),
        out_specs=P("wide", "narrow", None, None),
        check_vma=False,
    )
```

```python
import functools

import jax
import jax.numpy as jnp
from jax import lax
from jax.experimental import pallas as pl
from jax.experimental.pallas import tpu as pltpu
from jax.sharding import PartitionSpec as P

D = 1024
HEADS = 16
HD = 64
PD = 768
CLASSES = 16
TS = 16
TT = 256
CS = 4
UNSURE_MOST = 25
RECV = 7


EPS = 1e-06


def padded(cells, sides, width):
    for axis, dim in sides:
        count = lax.axis_size(axis)
        ends = count - 1
        head = lax.slice_in_dim(cells, 0, width, axis=dim)
        tail = lax.slice_in_dim(cells, cells.shape[dim] - width, cells.shape[dim], axis=dim)
        cells = jnp.concatenate(
            [
                lax.ppermute(tail, axis, [(i, (i + 1) % count) for i in range(ends)]),
                cells,
                lax.ppermute(head, axis, [((i + 1) % count, i) for i in range(ends)]),
            ],
            axis=dim,
        )
    return cells


def interp_table():
    fine = jnp.arange(TS, dtype=jnp.int32)
    eighths = 2 * fine - 3
    lower = eighths // 8
    frac = (eighths - 8 * lower).astype(jnp.float32) / 8.0
    column = jnp.arange(CS + 2, dtype=jnp.int32)
    left = (column[None, :] == (lower + 1)[:, None]).astype(jnp.float32)
    right = (column[None, :] == (lower + 2)[:, None]).astype(jnp.float32)
    return left * (1.0 - frac)[:, None] + right * frac[:, None]


def layer_norm(values, gain):
    center = values - jnp.mean(values, axis=-1, keepdims=True)
    spread = jnp.mean(center * center, axis=-1, keepdims=True)
    return center * lax.rsqrt(spread + EPS) * gain


RIM = 48
RIM_USED = (CS + 2) * (CS + 2)
LOG2E = 1.4426950408889634
VMEM_BYTES = 56 * 1024 * 1024


def dot(a, b):
    return jnp.dot(a, b, preferred_element_type=jnp.float32)


def dot_t(a, b):
    return lax.dot_general(a, b, (((1,), (1,)), ((), ())), preferred_element_type=jnp.float32)


def attend_tile(tokens, gain_ref, qkv_ref, out_ref, mixed_ref):
    normed = layer_norm(tokens, gain_ref[...]).astype(jnp.bfloat16)
    lane = lax.broadcasted_iota(jnp.int32, (TT, 2 * HD), 1)
    first = lane < HD
    ones_a = jnp.where(first, 1.0, 0.0).astype(jnp.bfloat16)
    ones_b = jnp.where(first, 0.0, 1.0).astype(jnp.bfloat16)
    zero = jnp.zeros((TT, 2 * HD), jnp.bfloat16)
    wide = 4 * HD
    for group in range(D // wide):
        at = group * wide
        q = dot(normed, qkv_ref[:, at : at + wide]).astype(jnp.bfloat16)
        k = dot(normed, qkv_ref[:, D + at : D + at + wide]).astype(jnp.bfloat16)
        v = dot(normed, qkv_ref[:, 2 * D + at : 2 * D + at + wide]).astype(jnp.bfloat16)
        for pair in range(2):
            cols = slice(pair * 2 * HD, (pair + 1) * 2 * HD)
            q2, k2, v2 = q[:, cols], k[:, cols], v[:, cols]
            parts = []
            for mine in (first, ~first):
                s = dot_t(jnp.where(mine, q2, zero), k2)
                top = jnp.max(s, axis=-1, keepdims=True)
                parts.append(jnp.exp2((s - top) * (LOG2E * HD ** (-0.5))).astype(jnp.bfloat16))
            p = jnp.concatenate(parts, axis=1)
            upper = jnp.concatenate([jnp.where(first, v2, zero), ones_a], axis=1)
            lower = jnp.concatenate([jnp.where(first, zero, v2), ones_b], axis=1)
            o = dot(p, jnp.concatenate([upper, lower], axis=0))
            mixed_ref[:, at + pair * 2 * HD : at + (pair + 1) * 2 * HD] = (
                o[:, : 2 * HD] / o[:, 2 * HD :]
            ).astype(jnp.bfloat16)
    return tokens + dot(mixed_ref[...], out_ref[...])


def glance_kernel(px_ref, patch_ref, pos_ref, gain_ref, qkv_ref, out_ref, feat_ref, mixed_ref):
    patches = px_ref[...].reshape(TT, PD)
    embed = dot(patches, patch_ref[...]) + pos_ref[...].astype(jnp.float32)
    result = attend_tile(embed, gain_ref, qkv_ref, out_ref, mixed_ref)
    feat_ref[...] = result.astype(jnp.bfloat16).reshape(feat_ref.shape)


def fixed(shape):
    return pl.BlockSpec(
        shape, lambda *_: (0,) * len(shape), pipeline_mode=pl.Buffered(1)
    )


def glance(coarse, patch_weight, position, gain_attn, qkv_weight, out_weight):
    rows, cols, _ = coarse.shape
    count = (rows // TS) * (cols // TS)
    return pl.pallas_call(
        glance_kernel,
        grid=(rows // TS, cols // TS),
        in_specs=[
            pl.BlockSpec((TS, TS, PD), lambda a, b: (a, b, 0)),
            fixed((PD, D)),
            fixed((TT, D)),
            fixed((1, D)),
            fixed((D, 3 * D)),
            fixed((D, D)),
        ],
        out_specs=pl.BlockSpec((TS, TS, D), lambda a, b: (a, b, 0)),
        out_shape=jax.ShapeDtypeStruct((rows, cols, D), jnp.bfloat16),
        scratch_shapes=[pltpu.VMEM((TT, D), jnp.bfloat16)],
        compiler_params=pltpu.CompilerParams(vmem_limit_bytes=VMEM_BYTES),
        cost_estimate=pl.CostEstimate(
            flops=count * 4_000_000_000, bytes_accessed=14_000_000, transcendentals=0
        ),
    )(coarse, patch_weight, position, gain_attn.reshape(1, D), qkv_weight, out_weight)


def source_specs(sizes, count, shape):
    specs = []
    for s in range(len(sizes)):
        specs.append(
            pl.BlockSpec((1,) + shape, lambda i, meta, s=s: (meta[(s + 1) * count + i], 0, 0))
        )
    return specs


def source_meta(entries, sizes):
    which = jnp.zeros_like(entries)
    blocks = []
    start = 0
    for size in sizes:
        if start:
            which = which + (entries >= start)
        blocks.append(jnp.clip(entries - start, 0, size - 1))
        start += size
    return jnp.concatenate([which.astype(jnp.int32)] + blocks).astype(jnp.int32)


def gather_kernel(meta_ref, *refs):
    out_ref = refs[-1]
    i = pl.program_id(0)
    for s, ref in enumerate(refs[:-1]):

        @pl.when(meta_ref[i] == s)
        def _(ref=ref):
            out_ref[...] = ref[...]


def gather_entries(sources, entries):
    sizes = [source.shape[0] for source in sources]
    count = entries.shape[0]
    shape = sources[0].shape[1:]
    moved = 2 * count * shape[0] * shape[1] * 2
    return pl.pallas_call(
        gather_kernel,
        grid_spec=pltpu.PrefetchScalarGridSpec(
            num_scalar_prefetch=1,
            grid=(count,),
            in_specs=source_specs(sizes, count, shape),
            out_specs=pl.BlockSpec((1,) + shape, lambda i, meta: (i, 0, 0)),
        ),
        out_shape=jax.ShapeDtypeStruct((count,) + shape, jnp.bfloat16),
        compiler_params=pltpu.CompilerParams(vmem_limit_bytes=VMEM_BYTES),
        cost_estimate=pl.CostEstimate(flops=0, bytes_accessed=moved, transcendentals=0),
    )(source_meta(entries, sizes), *sources)


def focus_kernel(sources, most, meta_ref, *refs):
    pixel_refs, rim_refs = refs[:sources], refs[sources : 2 * sources]
    (
        lift_ref,
        patch_ref,
        join_ref,
        pos_ref,
        gain_ref,
        qkv_ref,
        out_ref,
        gain_head_ref,
        head_ref,
        answer_ref,
        px_ref,
        rim_ref,
        mixed_ref,
    ) = refs[2 * sources :]
    i = pl.program_id(0)
    for s in range(sources):

        @pl.when(meta_ref[i] == s)
        def _(s=s):
            px_ref[...] = pixel_refs[s][0]
            rim_ref[...] = rim_refs[s][0]

    @pl.when(i < meta_ref[(sources + 1) * most])
    def _():
        joined = dot(rim_ref[...], join_ref[...])
        high = joined.astype(jnp.bfloat16)
        low = (joined - high.astype(jnp.float32)).astype(jnp.bfloat16)
        embed = dot(px_ref[...], patch_ref[...])
        embed = embed + dot(lift_ref[...], jnp.concatenate([high, low], axis=0))
        embed = embed + pos_ref[...].astype(jnp.float32)
        result = attend_tile(embed, gain_ref, qkv_ref, out_ref, mixed_ref)
        normed = layer_norm(result, gain_head_ref[...]).astype(jnp.bfloat16)
        answer_ref[0] = dot_t(head_ref[...], normed).astype(jnp.bfloat16)


def focus(entries, count, pixels, rims, lift, weights, expected):
    patch_weight, join_weight, position, gain_attn, qkv_weight, out_weight, gain_head, head_t = weights
    most = entries.shape[0]
    sizes = [source.shape[0] for source in pixels]
    meta = jnp.concatenate([source_meta(entries, sizes), count.reshape(1)])
    return pl.pallas_call(
        functools.partial(focus_kernel, len(sizes), most),
        grid_spec=pltpu.PrefetchScalarGridSpec(
            num_scalar_prefetch=1,
            grid=(most,),
            in_specs=source_specs(sizes, most, (TT, PD))
            + source_specs(sizes, most, (RIM, D))
            + [
                fixed((TT, 2 * RIM)),
                fixed((PD, D)),
                fixed((D, D)),
                fixed((TT, D)),
                fixed((1, D)),
                fixed((D, 3 * D)),
                fixed((D, D)),
                fixed((1, D)),
                fixed((CLASSES, D)),
            ],
            out_specs=pl.BlockSpec((1, CLASSES, TT), lambda i, meta: (i, 0, 0)),
            scratch_shapes=[
                pltpu.VMEM((TT, PD), jnp.bfloat16),
                pltpu.VMEM((RIM, D), jnp.bfloat16),
                pltpu.VMEM((TT, D), jnp.bfloat16),
            ],
        ),
        out_shape=jax.ShapeDtypeStruct((most, CLASSES, TT), jnp.bfloat16),
        compiler_params=pltpu.CompilerParams(vmem_limit_bytes=VMEM_BYTES),
        cost_estimate=pl.CostEstimate(
            flops=expected * 7_000_000_000, bytes_accessed=14_000_000, transcendentals=0
        ),
    )(
        meta,
        *pixels,
        *rims,
        lift,
        patch_weight,
        join_weight,
        position,
        gain_attn.reshape(1, D),
        qkv_weight,
        out_weight,
        gain_head.reshape(1, D),
        head_t,
    )


def before_each(x):
    return jnp.cumsum(x) - x


def listed(held, order, count):
    slots = jnp.arange(count, dtype=jnp.int32)
    match = (held[None, :] == 1) & (order[None, :] == slots[:, None])
    ids = jnp.arange(held.shape[0], dtype=jnp.int32)
    return jnp.sum(match * ids[None, :], axis=1).astype(jnp.int32)


def swapped_pairs(x):
    return x.reshape(-1, 2)[:, ::-1].reshape(-1)


def first_moves(loads, most):
    sums = loads.reshape(-1, 2).sum(axis=1)
    odd = sums % 2
    extra = before_each(odd) % 2
    side = jnp.arange(2, dtype=jnp.int32)[None, :]
    share = sums[:, None] // 2 + odd[:, None] * (side == extra[:, None])
    return jnp.clip(loads - share.reshape(-1), 0, most)


def second_moves(loads, most):
    sides = loads.reshape(-1, 2).T
    n = sides.shape[1]
    share = (jnp.sum(sides, axis=1, keepdims=True) + n - 1) // n
    over = jnp.maximum(sides - share, 0)
    under = jnp.maximum(share - sides, 0)
    over_at = jnp.cumsum(over, axis=1) - over
    under_at = jnp.cumsum(under, axis=1) - under
    ends = jnp.minimum((over_at + over)[:, :, None], (under_at + under)[:, None, :])
    starts = jnp.maximum(over_at[:, :, None], under_at[:, None, :])
    return jnp.clip(ends - starts, 0, most)


def lift_table():
    table = interp_table()
    both = (table[:, None, :, None] * table[None, :, None, :]).reshape(TT, RIM_USED)
    return jnp.pad(both, ((0, 0), (0, RIM - RIM_USED))).astype(jnp.bfloat16)


def rim_cells(tiles, tile_cols, cols):
    k = jnp.arange(RIM, dtype=jnp.int32)
    cell = (tiles // tile_cols * CS)[:, None] + k[None, :] // (CS + 2)
    cell = cell * cols + (tiles % tile_cols * CS)[:, None] + k[None, :] % (CS + 2)
    return jnp.where(k[None, :] < RIM_USED, cell, -1)


def wide_edges(features):
    bordered = padded(features, (("wide", 0),), 1)
    wide_pos = lax.axis_index("wide")
    top_row = jnp.where(wide_pos == 0, bordered[1:2], bordered[0:1])
    bottom_row = jnp.where(
        wide_pos == lax.axis_size("wide") - 1, bordered[-2:-1], bordered[-1:]
    )
    return jnp.concatenate([top_row, bordered[1:-1], bottom_row], axis=0)


def narrow_edges(rows):
    bordered = padded(rows, (("narrow", 1),), 1)
    narrow_pos = lax.axis_index("narrow")
    left_col = jnp.where(narrow_pos == 0, bordered[:, 1:2], bordered[:, 0:1])
    right_col = jnp.where(
        narrow_pos == lax.axis_size("narrow") - 1, bordered[:, -2:-1], bordered[:, -1:]
    )
    bordered = jnp.concatenate([left_col, bordered[:, 1:-1], right_col], axis=1)
    return bordered


def glance_answer(flat, gain_head, head_weight, cells, lift):
    tile_count = cells.shape[0]
    normed = layer_norm(flat.astype(jnp.float32), gain_head).astype(jnp.bfloat16)
    coarse = lax.dot_general(
        head_weight, normed, (((0,), (1,)), ((), ())), preferred_element_type=jnp.float32
    )
    pieces = []
    for _ in range(3):
        piece = lax.reduce_precision(coarse, 8, 7)
        pieces.append(piece.astype(jnp.bfloat16))
        coarse = coarse - piece
    stacked = jnp.concatenate(pieces, axis=0)
    chosen = (
        jnp.arange(flat.shape[0], dtype=jnp.int32)[:, None] == cells.reshape(1, -1)
    ).astype(jnp.bfloat16)
    rim_logits = dot(stacked, chosen).astype(jnp.bfloat16).reshape(3 * CLASSES * tile_count, RIM)
    fine = dot_t(rim_logits, lift).reshape(3, CLASSES, tile_count, TT)
    return (fine[0] + fine[1] + fine[2]).astype(jnp.bfloat16).transpose(1, 0, 2)


def per_device(
    pixels,
    coarse_pixels,
    unsure,
    patch_weight,
    position,
    qkv_weight,
    out_weight,
    join_weight,
    gain_attn,
    gain_head,
    head_weight,
):
    tile_rows, tile_cols = unsure.shape
    tile_count = tile_rows * tile_cols
    wide_len = lax.axis_size("wide")
    me = lax.axis_index("wide")
    pairs = wide_len // 2
    first_most = UNSURE_MOST // 2 - 1
    second_most = -(-(UNSURE_MOST // 2) // pairs)
    masks = list(range(1, pairs))
    second_slots = len(masks) * second_most
    flags = unsure.reshape(-1)
    flat_pixels = pixels.reshape(tile_count, TT, PD)
    loads = lax.all_gather(jnp.sum(flags), "wide")

    def swap(x, mask):
        return lax.ppermute(x, "wide", [(i, i ^ mask) for i in range(wide_len)])

    moves = first_moves(loads, first_most)
    order = before_each(flags)
    given = moves[me]
    taken = moves[me ^ 1]
    sent = flags * (order < given)
    first_entries = listed(sent, order, first_most)
    first_back = order
    sending = gather_entries([flat_pixels], first_entries)
    sending, coarse_pixels = lax.optimization_barrier((sending, coarse_pixels))
    first_pixels = swap(sending, 1)

    loads = loads - moves + swapped_pairs(moves)
    moves = second_moves(loads, second_most)
    side, pair = me % 2, me // 2
    out_moves = jnp.stack([moves[side, pair, pair ^ m] for m in masks])
    in_moves = jnp.stack([moves[side, pair ^ m, pair] for m in masks])
    held = jnp.concatenate(
        [flags - sent, (jnp.arange(first_most, dtype=jnp.int32) < taken).astype(jnp.int32)]
    )
    rank = before_each(held)
    step = jnp.arange(second_most, dtype=jnp.int32)[None, :]
    slot_rank = jnp.where(
        step < out_moves[:, None], before_each(out_moves)[:, None] + step, -1
    ).reshape(-1)
    match = ((held[None, :] == 1) & (rank[None, :] == slot_rank[:, None])).astype(jnp.int32)
    entry_ids = jnp.arange(held.shape[0], dtype=jnp.int32)
    slot_ids = jnp.arange(second_slots, dtype=jnp.int32)
    second_entries = jnp.sum(match * entry_ids[None, :], axis=1)
    second_back = jnp.sum(match * slot_ids[:, None], axis=0)
    gone = jnp.sum(match, axis=0)
    kept = held - gone
    kept_order = before_each(kept)
    kept_entries = listed(kept, kept_order, UNSURE_MOST)
    arrived = (step < in_moves[:, None]).astype(jnp.int32).reshape(-1)
    arrived_order = before_each(arrived)
    arrived_entries = listed(arrived, arrived_order, second_slots)

    def spread(sending):
        parts = sending.reshape((len(masks), second_most) + sending.shape[1:])
        return [swap(parts[k], 2 * m) for k, m in enumerate(masks)]

    features = glance(coarse_pixels, patch_weight, position, gain_attn, qkv_weight, out_weight)
    bordered = wide_edges(features)
    bordered, first_pixels, second_entries = lax.optimization_barrier(
        (bordered, first_pixels, second_entries)
    )
    sending = gather_entries([flat_pixels, first_pixels], second_entries)
    bordered, sending = lax.optimization_barrier((bordered, sending))
    second_pixels = spread(sending)
    bordered = narrow_edges(bordered)
    cols = bordered.shape[1]
    flat = bordered.reshape(-1, D)
    lift = lift_table()
    cells = rim_cells(jnp.arange(tile_count, dtype=jnp.int32), tile_cols, cols)
    chosen = (
        cells.reshape(-1)[:, None] == jnp.arange(flat.shape[0], dtype=jnp.int32)[None, :]
    ).astype(jnp.bfloat16)
    rims = dot(chosen, flat).astype(jnp.bfloat16).reshape(tile_count, RIM, D)
    first_rims = swap(gather_entries([rims], first_entries), 1)
    second_rims = spread(gather_entries([rims, first_rims], second_entries))
    glance_logits = glance_answer(flat, gain_head, head_weight, cells, lift)
    weights = (
        patch_weight,
        join_weight,
        position,
        gain_attn,
        qkv_weight,
        out_weight,
        gain_head,
        head_weight.T,
    )
    twice = jnp.concatenate([lift, lift], axis=1)
    usual = RECV + 1
    kept_count = jnp.sum(kept)
    kept_pixels, kept_rims = [flat_pixels, first_pixels], [rims, first_rims]
    kept_answer = focus(
        kept_entries[:usual], kept_count, kept_pixels, kept_rims, twice, weights, 4
    )
    more_answer = lax.cond(
        kept_count > usual,
        lambda: focus(
            kept_entries[usual:], kept_count - usual, kept_pixels, kept_rims, twice, weights, 1
        ),
        lambda: jnp.zeros((UNSURE_MOST - usual, CLASSES, TT), jnp.bfloat16),
    )
    arrived_answer = focus(
        arrived_entries, jnp.sum(arrived), second_pixels, second_rims, twice, weights, 3
    )

    back = arrived_answer[arrived_order].reshape(len(masks), second_most, CLASSES, TT)
    answers = jnp.concatenate(
        [kept_answer, more_answer] + [swap(back[k], 2 * m) for k, m in enumerate(masks)], axis=0
    )
    place = jnp.where(gone == 1, UNSURE_MOST + second_back, kept_order)
    place = jnp.clip(place, 0, answers.shape[0] - 1)
    returned = swap(answers[place[tile_count:]], 1)
    place = jnp.where(sent == 1, answers.shape[0] + first_back, place[:tile_count])
    answers = jnp.concatenate([answers, returned], axis=0)
    focused = answers[jnp.clip(place, 0, answers.shape[0] - 1)]
    result = jnp.where(flags[:, None, None] == 1, focused, glance_logits)
    return result.reshape(tile_rows, tile_cols, CLASSES, TT)


def solution(mesh):
    return jax.shard_map(
        per_device,
        mesh=mesh,
        in_specs=(
            P("wide", "narrow", None, None),
            P("wide", "narrow", None),
            P("wide", "narrow"),
            P(),
            P(),
            P(),
            P(),
            P(),
            P(),
            P(),
            P(),
        ),
        out_specs=P("wide", "narrow", None, None),
        check_vma=False,
    )
```
